32 devices in a mesh: rows: 8 (over z, y), panel: 4 (over x, core).
Axes of the slice: x: 2, y: 2, z: 4, core: 2. Of those that a mesh axis runs over, the one named last changes fastest.
Arguments:
- pair_block: bfloat16 [2048, 16384], P('rows', 'panel'), may hold values from -6 to 6
- resolvent: float32 [16384, 16384], P('panel', 'rows'), may hold values from -0.046875 to 0.046875
- virt_coef: bfloat16 [1024, 11200], P('rows', 'panel'), may hold values from -0.1875 to 0.1875
- slot_row: int32 [2048], replicated, may hold values from 0 to 2047, each once
Outputs:
- backward: float32 [2, 11200, 16384], P(None, 'panel', 'rows')
The draws below stay inside these ranges and needn't reach their ends.
Inputs may be any that keep to these rules, and one draw needn't show every extreme that they name: `slot_row`: every pair row appears exactly once.
All inputs are finite; a program needn't handle non-finite values.
Results may differ from the reference program's by a relative error of at most 0.0041.
Values may be sent and summed in bfloat16 or wider, within the bound.
No kernel may reach another device: no remote copies, remote signals or barrier semaphores. Data moves between devices by JAX's collectives and lax.ppermute only.
A program may use at most 192 MiB of HBM per device.

```python
import jax
import jax.numpy as jnp

NAUX = 16384
NAO = 11200
PAIRS = 2048
OCC_B = 2
VW = 1024


def levels(own_key, dims, pieces, smallest, top_value):
    loudness = 1.0
    for dim, shards_of in pieces:
        draws = jax.random.uniform(jax.random.fold_in(jax.random.fold_in(own_key, 6), dim), (shards_of,), jnp.float32, smallest / len(pieces), top_value / len(pieces))
        loudness = loudness * jnp.repeat(jnp.exp(draws), dims[dim] // shards_of).reshape((-1,) + (1,) * (len(dims) - 1 - dim))
    return loudness


def noise(stream_key, dims, deviation, limit, shards=(), kind=jnp.bfloat16):
    drawn = deviation * jax.random.normal(stream_key, dims, jnp.float32)
    if shards:
        drawn = drawn * levels(stream_key, dims, shards, -0.22, 0.18)
    return jnp.clip(drawn, -limit, limit).astype(kind)


def setup_inputs(seed: int = 0) -> dict:
    seeds = jax.random.split(jax.random.key(seed), 5)
    pair_block = noise(seeds[0], (PAIRS, NAUX), 1.0, 6.0, ((0, 8), (1, 4)))
    resolvent = noise(seeds[1], (NAUX, NAUX), NAUX ** -0.5, 0.046875, ((0, 4), (1, 8)), jnp.float32)
    virt_coef = noise(seeds[2], (VW, NAO), VW ** -0.5, 0.1875, ((0, 8), (1, 4)))
    slot_row = jax.random.permutation(seeds[3], PAIRS).astype(jnp.int32)
    return {"pair_block": pair_block, "resolvent": resolvent, "virt_coef": virt_coef, "slot_row": slot_row}


def reference(pair_block, resolvent, virt_coef, slot_row):
    resolvent_round = resolvent.astype(jnp.bfloat16)
    gamma = jnp.dot(pair_block, resolvent_round, preferred_element_type=jnp.float32)
    gamma_round = gamma.astype(jnp.bfloat16)
    grouped = jnp.take(gamma_round, slot_row.astype(jnp.int32), axis=0)
    grouped = grouped.reshape(OCC_B, PAIRS // OCC_B, gamma.shape[1])
    return jnp.einsum("am,oac->omc", virt_coef.astype(jnp.float32), grouped.astype(jnp.float32))
```

```python
import functools

import jax
import jax.numpy as jnp
from jax import lax
from jax.experimental import pallas as pl
from jax.experimental.pallas import tpu as pltpu
from jax.sharding import PartitionSpec as P

OCC_B = 2
LAGS = (None, None, 1, None)
VMEM_LIMIT = 56 * 1024 * 1024
BF16, F32 = jnp.bfloat16, jnp.float32


def divisor_tile(size, step, top):
    best = [t for t in range(step, min(size, top) + 1, step) if size % t == 0]
    return best[-1] if best else size


def bit_reversed(n):
    order = [0]
    while len(order) < n:
        order = [2 * j for j in order] + [2 * j + 1 for j in order]
    return order


def params():
    return pltpu.CompilerParams(
        dimension_semantics=("arbitrary",), vmem_limit_bytes=VMEM_LIMIT
    )


def split_store(res, keep_ref, send_ref, place, order):
    part = res.shape[0] // len(order)
    half = max(len(order) // 2, 1)
    for slot, j in enumerate(order):
        rows = res[pl.ds(pl.multiple_of((place ^ j) * part, part), part), :]
        if slot < half:
            keep_ref[slot * part : (slot + 1) * part, :] = rows
        else:
            send_ref[(slot - half) * part : (slot - half + 1) * part, :] = rows


def first_kernel(order, place_ref, lhs_ref, r_ref, r16_ref, keep_ref, send_ref, res):
    r16_ref[...] = r_ref[...].astype(BF16)
    res[...] = jnp.dot(lhs_ref[...], r16_ref[...], preferred_element_type=F32)
    split_store(res, keep_ref, send_ref, place_ref[0], order)


def first_product(place, lhs, resolvent, order):
    rows, depth = lhs.shape
    cols = resolvent.shape[1]
    tile = divisor_tile(cols, 128, 256)
    half = rows // 2
    return pl.pallas_call(
        functools.partial(first_kernel, order),
        grid_spec=pltpu.PrefetchScalarGridSpec(
            num_scalar_prefetch=1,
            grid=(cols // tile,),
            in_specs=[
                pl.BlockSpec((rows, depth), lambda i, s: (0, 0)),
                pl.BlockSpec((depth, tile), lambda i, s: (0, i)),
            ],
            out_specs=[
                pl.BlockSpec((depth, tile), lambda i, s: (0, i)),
                pl.BlockSpec((half, tile), lambda i, s: (0, i)),
                pl.BlockSpec((half, tile), lambda i, s: (0, i)),
            ],
            scratch_shapes=[pltpu.VMEM((rows, tile), F32)],
        ),
        out_shape=[
            jax.ShapeDtypeStruct((depth, cols), BF16),
            jax.ShapeDtypeStruct((half, cols), F32),
            jax.ShapeDtypeStruct((half, cols), F32),
        ],
        compiler_params=params(),
        cost_estimate=pl.CostEstimate(
            flops=0, bytes_accessed=0, transcendentals=0
        ),
        name="first_product",
    )(place, lhs, resolvent)


def group_kernel(n, order, place_ref, *refs):
    pieces, (r_ref, keep_ref, send_ref, lhs, res) = refs[:n], refs[n:]

    @pl.when(pl.program_id(0) == 0)
    def _():
        at = 0
        for piece in pieces:
            lhs[at : at + piece.shape[0], :] = piece[...]
            at += piece.shape[0]

    res[...] = jnp.dot(lhs[...], r_ref[...], preferred_element_type=F32)
    split_store(res, keep_ref, send_ref, place_ref[0], order)


def group_product(place, pieces, r16, order):
    rows = sum(piece.shape[0] for piece in pieces)
    depth, cols = r16.shape
    tile = divisor_tile(cols, 128, 512)
    half = rows // 2
    return pl.pallas_call(
        functools.partial(group_kernel, len(pieces), order),
        grid_spec=pltpu.PrefetchScalarGridSpec(
            num_scalar_prefetch=1,
            grid=(cols // tile,),
            in_specs=[pl.BlockSpec(piece.shape, lambda i, s: (0, 0)) for piece in pieces]
            + [pl.BlockSpec((depth, tile), lambda i, s: (0, i))],
            out_specs=[
                pl.BlockSpec((half, tile), lambda i, s: (0, i)),
                pl.BlockSpec((half, tile), lambda i, s: (0, i)),
            ],
            scratch_shapes=[pltpu.VMEM((rows, depth), BF16), pltpu.VMEM((rows, tile), F32)],
        ),
        out_shape=[jax.ShapeDtypeStruct((half, cols), F32)] * 2,
        compiler_params=params(),
        cost_estimate=pl.CostEstimate(
            flops=0, bytes_accessed=0, transcendentals=0
        ),
        name="group_product",
    )(place, *pieces, r16)


def back_kernel(n, m, *refs):
    coefs, refs = refs[:n], refs[n:]
    if m:
        slots_ref, ids, gammas, refs = refs[0], refs[1 : 1 + m], refs[1 + m : 1 + 2 * m], refs[1 + 2 * m :]
        g_ref, out_ref, whole_ref, lhs, picks = refs
    else:
        g_ref, _, out_ref, lhs = refs
        whole_ref = g_ref
    occ, depth, tile = g_ref.shape

    @pl.when(pl.program_id(0) == 0)
    def _():
        at = 0
        for c in coefs:
            lhs[:, at : at + c.shape[1]] = c[...]
            at += c.shape[1]
        at = 0
        for i in range(m):
            wide = ids[i].shape[1]
            picks[:, at : at + wide] = (slots_ref[...] == ids[i][...]).astype(F32).astype(BF16)
            at += wide

    for o in range(occ):
        if m:
            placed = g_ref[o].astype(F32)
            at = 0
            for i in range(m):
                wide = ids[i].shape[1]
                placed += jnp.dot(
                    picks[o * depth : (o + 1) * depth, at : at + wide],
                    gammas[i][...],
                    preferred_element_type=F32,
                )
                at += wide
            whole_ref[o] = placed.astype(BF16)
        out_ref[o] = jnp.dot(lhs[...], whole_ref[o], preferred_element_type=F32)


def back_product(coefs, late, grouped, total, first, out):
    chunk = coefs[0].shape[0]
    occ, depth, cols = grouped.shape
    tile = divisor_tile(cols, 128, 256)
    n, m = len(coefs), 0
    at_col = lambda i: (0, 0, i)
    specs = [pl.BlockSpec(c.shape, lambda i: (0, 0)) for c in coefs]
    whole = (pl.Element(occ), pl.Element(chunk), pl.Element(tile))
    out_specs = [pl.BlockSpec(whole, lambda i: (0, first, i * tile))]
    shapes = [jax.ShapeDtypeStruct((occ, total, cols), F32)]
    scratch = [pltpu.VMEM((chunk, depth), BF16)]
    args = list(coefs)
    aliases = {}
    if late is not None:
        slots, ids, gammas = late
        m = len(ids)
        args += [slots, *ids, *gammas, grouped]
        specs += [pl.BlockSpec(slots.shape, lambda i: (0, 0))]
        specs += [pl.BlockSpec(v.shape, lambda i: (0, 0)) for v in ids]
        specs += [pl.BlockSpec((g.shape[0], tile), lambda i: (0, i)) for g in gammas]
        specs += [pl.BlockSpec((occ, depth, tile), at_col)]
        out_specs.append(pl.BlockSpec((occ, depth, tile), at_col))
        shapes.append(jax.ShapeDtypeStruct(grouped.shape, BF16))
        scratch.append(pltpu.VMEM((occ * depth, sum(v.shape[1] for v in ids)), BF16))
    else:
        args += [grouped, out]
        specs += [pl.BlockSpec((occ, depth, tile), at_col), pl.BlockSpec(memory_space=pl.ANY)]
        aliases = {len(args) - 1: 0}
    return pl.pallas_call(
        functools.partial(back_kernel, n, m),
        grid=(cols // tile,),
        in_specs=specs,
        out_specs=out_specs,
        out_shape=shapes,
        scratch_shapes=scratch,
        input_output_aliases=aliases,
        compiler_params=params(),
        cost_estimate=pl.CostEstimate(
            flops=0, bytes_accessed=0, transcendentals=0
        ),
        name="back_product",
    )(*args)


def tied(value, *after):
    return lax.optimization_barrier((value, *after))[0]


def body(rows, panel, pair_block, resolvent, virt_coef, slot_row):
    high = rows // 2
    up = [(r, (r + 2) % rows) for r in range(rows)]
    down = [(r, (r - 2) % rows) for r in range(rows)]
    swap = [(r, r ^ 1) for r in range(rows)]
    me_row, me_panel = lax.axis_index("rows"), lax.axis_index("panel")
    order = bit_reversed(panel)
    place = me_panel.astype(jnp.int32).reshape(1)
    stages = [1 << k for k in range((panel - 1).bit_length())]

    def over_rows(v, pairs):
        return lax.ppermute(v, "rows", pairs)

    def over_panel(v, width):
        return lax.ppermute(v, "panel", [(q, q ^ width) for q in range(panel)])

    def block_of(s, cross):
        return (me_row // 2 + (high - s)) % high * 2 + ((me_row % 2) ^ cross)

    def spread(pieces, fence):
        straight = [dict(enumerate(pieces))]
        crossed = []
        arrivals = []
        for s in range(high - 1):
            straight.append({})
            crossed.append({})
            for c in range(2):
                got = [over_rows(straight[s][c], up), over_rows(straight[s][c], swap)]
                straight[s + 1][c], crossed[s][c] = got = fence(got)
                arrivals.append([((s + 1, 0, c), got[0]), ((s, 1, c), got[1])])
        s = high - 1
        ends = [over_rows(straight[s][0], swap)]
        if high > 1:
            ends.append(over_rows(tied(crossed[0][1], straight[s][0]), down))
        else:
            ends.append(over_rows(straight[s][1], swap))
        ends = fence(ends)
        arrivals.append([((s, 1, c), ends[c]) for c in range(2)])
        return arrivals

    vblock = virt_coef.shape[0]
    sequence = [(0, 0)] + [
        key for s in range(high) for key in ([(s + 1, 0)] if s < high - 1 else []) + [(s, 1)]
    ]
    by_block = slot_row.reshape(OCC_B, rows, vblock)
    slots = jnp.concatenate(
        [lax.dynamic_slice_in_dim(by_block, block_of(*key), 1, axis=1) for key in sequence], axis=1
    ).reshape(-1, 1)

    size = pair_block.shape[0]
    step = size // 2

    def row_ids(keys):
        natural = jnp.concatenate(
            [block_of(s, x) * size + c * step + jnp.arange(step, dtype=jnp.int32) for s, x, c in keys]
        )
        cut_ids = natural.reshape(panel, -1)
        return jnp.concatenate([cut_ids[me_panel ^ j] for j in order]).reshape(1, -1)

    parts, sums, owns, gammas, ids = [], [], [], [], []

    def panel_sum(keep, send, keys):
        parts.append(send)
        for k, width in enumerate(stages):
            got = over_panel(send, width)
            if k + 1 < len(stages):
                half = keep.shape[0] // 2
                send = keep[half:] + got[half:]
                keep = (keep[:half], got[:half])
                sums.append(send) if k == 0 else None
                keep = keep[0] + keep[1]
            else:
                keep = keep + got
        own = keep.astype(BF16)
        owns.append(own)
        for width in reversed(stages):
            own = jnp.concatenate([own, over_panel(own, width)], axis=0)
        gammas.append(own)
        ids.append(row_ids(keys))

    def regroup(grouped, which):
        gamma = jnp.concatenate([gammas[k] for k in which], axis=0)
        pick = (slots == jnp.concatenate([ids[k] for k in which], axis=1)).astype(BF16)
        placed = jnp.dot(pick, gamma, preferred_element_type=F32)
        if grouped is not None:
            placed = placed + grouped.astype(F32)
        return placed.astype(BF16)

    piece0 = pair_block[:step]
    piece1 = tied(pair_block, piece0)[step:]
    r16, keep, send = first_product(place, pair_block, resolvent, order)
    panel_sum(keep, send, [(0, 0, 0), (0, 0, 1)])
    grouped = None
    count = 2 * (high - 1) + 1
    batch = max(1, 512 // (2 * step))
    closing = [len(range(0, h + 1)) for h in range(count)]
    closes = {h for h in range(count) if h >= count - 3 or (h + 1) % batch == 0 or h == count - 4}
    pending = []
    marks = []

    def fence(got):
        h = len(marks)
        after = []
        if h:
            for kind, lag in zip((parts, sums, owns, gammas), LAGS):
                if lag is not None and len(kind) > lag:
                    after.append(kind[-1 - lag])
        got = list(lax.optimization_barrier((*got, *after)))[: len(got)]
        marks.append(got[0])
        return got

    coef_at = max(count - 2, 0)
    arrivals = None

    state = {"grouped": None}

    def take(h, items):
        pending.extend(items)
        if h not in closes:
            return
        keep, send = group_product(place, [v for _, v in pending], r16, order)
        panel_sum(keep, send, [key for key, _ in pending])
        pending.clear()
        k = len(gammas) - 1
        if k >= 3 and k % 2:
            state["grouped"] = regroup(state["grouped"], [k - 3, k - 2])

    straight = [{0: piece0, 1: piece1}]
    crossed = []
    h = 0
    for s in range(high - 1):
        straight.append({})
        crossed.append({})
        for c in range(2):
            got = fence([over_rows(straight[s][c], up), over_rows(straight[s][c], swap)])
            straight[s + 1][c], crossed[s][c] = got
            take(h, [((s + 1, 0, c), got[0]), ((s, 1, c), got[1])])
            h += 1
    s = high - 1
    ends = [over_rows(straight[s][0], swap)]
    if high > 1:
        ends.append(over_rows(tied(crossed[0][1], straight[s][0]), down))
    else:
        ends.append(over_rows(straight[s][1], swap))
    ends = fence(ends)
    take(h, [((s, 1, c), ends[c]) for c in range(2)])

    done = len(gammas) - 2 if len(gammas) % 2 == 0 else len(gammas) - 1
    late = list(range(0 if state["grouped"] is None else done, len(gammas)))
    grouped = state["grouped"]
    if grouped is None:
        grouped = jnp.zeros((slots.shape[0], gammas[0].shape[1]), BF16)

    coef = tied(virt_coef, marks[max(len(marks) - 2, 0)]).T
    total = coef.shape[0]
    cut = divisor_tile(total, 16, total // 2)
    cut = total // 16 // 2 * 16
    arrived = [{}, {}]
    for items in spread([coef[:cut], coef[cut:]], lambda got: got):
        for (back, x, c), v in items:
            arrived[c][(back, x)] = v
    arrived[0][(0, 0)], arrived[1][(0, 0)] = coef[:cut], coef[cut:]
    grouped = grouped.reshape(OCC_B, rows * vblock, -1)
    out = None
    for c, first in enumerate((0, cut)):
        parts = [arrived[c][key] for key in sequence]
        if vblock % 128:
            parts = [jnp.concatenate(parts, axis=1)]
        if c == 0:
            out, grouped = back_product(
                parts, (slots, [ids[k] for k in late], [gammas[k] for k in late]), grouped, total, first, None
            )
        else:
            (out,) = back_product(parts, None, grouped, total, first, out)
    return out


def solution(mesh):
    placed = (P("rows", "panel"), P("panel", "rows"), P("rows", "panel"), P())
    return jax.shard_map(
        functools.partial(body, mesh.shape["rows"], mesh.shape["panel"]),
        mesh=mesh,
        in_specs=placed,
        out_specs=P(None, "panel", "rows"),
        check_vma=False,
    )
```

```python
import functools

import jax
import jax.numpy as jnp
from jax import lax
from jax.experimental import pallas as pl
from jax.experimental.pallas import tpu as pltpu
from jax.sharding import PartitionSpec as P

OCC_B = 2
COEF_AT = 2
LAGS = (None, None, 1, None)
VMEM_LIMIT = 56 * 1024 * 1024
BF16, F32 = jnp.bfloat16, jnp.float32


def divisor_tile(size, step, top):
    best = [t for t in range(step, min(size, top) + 1, step) if size % t == 0]
    return best[-1] if best else size


def bit_reversed(n):
    order = [0]
    while len(order) < n:
        order = [2 * j for j in order] + [2 * j + 1 for j in order]
    return order


def params():
    return pltpu.CompilerParams(
        dimension_semantics=("arbitrary",), vmem_limit_bytes=VMEM_LIMIT
    )


def split_store(res, keep_ref, send_ref, place, order):
    part = res.shape[0] // len(order)
    half = max(len(order) // 2, 1)
    for slot, j in enumerate(order):
        rows = res[pl.ds(pl.multiple_of((place ^ j) * part, part), part), :]
        if slot < half:
            keep_ref[slot * part : (slot + 1) * part, :] = rows
        else:
            send_ref[(slot - half) * part : (slot - half + 1) * part, :] = rows


def first_kernel(order, place_ref, lhs_ref, r_ref, r16_ref, keep_ref, send_ref, res):
    r16_ref[...] = r_ref[...].astype(BF16)
    res[...] = jnp.dot(lhs_ref[...], r16_ref[...], preferred_element_type=F32)
    split_store(res, keep_ref, send_ref, place_ref[0], order)


def first_product(place, lhs, resolvent, order):
    rows, depth = lhs.shape
    cols = resolvent.shape[1]
    tile = divisor_tile(cols, 128, 256)
    half = rows // 2
    return pl.pallas_call(
        functools.partial(first_kernel, order),
        grid_spec=pltpu.PrefetchScalarGridSpec(
            num_scalar_prefetch=1,
            grid=(cols // tile,),
            in_specs=[
                pl.BlockSpec((rows, depth), lambda i, s: (0, 0)),
                pl.BlockSpec((depth, tile), lambda i, s: (0, i)),
            ],
            out_specs=[
                pl.BlockSpec((depth, tile), lambda i, s: (0, i)),
                pl.BlockSpec((half, tile), lambda i, s: (0, i)),
                pl.BlockSpec((half, tile), lambda i, s: (0, i)),
            ],
            scratch_shapes=[pltpu.VMEM((rows, tile), F32)],
        ),
        out_shape=[
            jax.ShapeDtypeStruct((depth, cols), BF16),
            jax.ShapeDtypeStruct((half, cols), F32),
            jax.ShapeDtypeStruct((half, cols), F32),
        ],
        compiler_params=params(),
        cost_estimate=pl.CostEstimate(
            flops=1000, bytes_accessed=1000, transcendentals=0
        ),
        name="first_product",
    )(place, lhs, resolvent)


def group_kernel(n, order, place_ref, *refs):
    pieces, (r_ref, keep_ref, send_ref, lhs, res) = refs[:n], refs[n:]

    @pl.when(pl.program_id(0) == 0)
    def _():
        at = 0
        for piece in pieces:
            lhs[at : at + piece.shape[0], :] = piece[...]
            at += piece.shape[0]

    res[...] = jnp.dot(lhs[...], r_ref[...], preferred_element_type=F32)
    split_store(res, keep_ref, send_ref, place_ref[0], order)


def group_product(place, pieces, r16, order):
    rows = sum(piece.shape[0] for piece in pieces)
    depth, cols = r16.shape
    tile = divisor_tile(cols, 128, 512)
    half = rows // 2
    return pl.pallas_call(
        functools.partial(group_kernel, len(pieces), order),
        grid_spec=pltpu.PrefetchScalarGridSpec(
            num_scalar_prefetch=1,
            grid=(cols // tile,),
            in_specs=[pl.BlockSpec(piece.shape, lambda i, s: (0, 0)) for piece in pieces]
            + [pl.BlockSpec((depth, tile), lambda i, s: (0, i))],
            out_specs=[
                pl.BlockSpec((half, tile), lambda i, s: (0, i)),
                pl.BlockSpec((half, tile), lambda i, s: (0, i)),
            ],
            scratch_shapes=[pltpu.VMEM((rows, depth), BF16), pltpu.VMEM((rows, tile), F32)],
        ),
        out_shape=[jax.ShapeDtypeStruct((half, cols), F32)] * 2,
        compiler_params=params(),
        cost_estimate=pl.CostEstimate(
            flops=1000, bytes_accessed=1000, transcendentals=0
        ),
        name="group_product",
    )(place, *pieces, r16)


def back_kernel(n, m, *refs):
    coefs, refs = refs[:n], refs[n:]
    if m:
        slots_ref, ids, gammas, refs = refs[0], refs[1 : 1 + m], refs[1 + m : 1 + 2 * m], refs[1 + 2 * m :]
        g_ref, out_ref, whole_ref, lhs, picks = refs
    else:
        g_ref, _, out_ref, lhs = refs
        whole_ref = g_ref
    occ, depth, tile = g_ref.shape

    @pl.when(pl.program_id(0) == 0)
    def _():
        at = 0
        for c in coefs if n > 1 else ():
            lhs[:, at : at + c.shape[1]] = c[...]
            at += c.shape[1]
        at = 0
        for i in range(m):
            wide = ids[i].shape[1]
            picks[:, at : at + wide] = (slots_ref[...] == ids[i][...]).astype(F32).astype(BF16)
            at += wide

    for o in range(occ):
        if m:
            placed = g_ref[o].astype(F32)
            at = 0
            for i in range(m):
                wide = ids[i].shape[1]
                placed += jnp.dot(
                    picks[o * depth : (o + 1) * depth, at : at + wide],
                    gammas[i][...],
                    preferred_element_type=F32,
                )
                at += wide
            whole_ref[o] = placed.astype(BF16)
        left = lhs if n > 1 else coefs[0]
        out_ref[o] = jnp.dot(left[...], whole_ref[o], preferred_element_type=F32)


def back_product(coefs, late, grouped, total, first, out):
    chunk = coefs[0].shape[0]
    occ, depth, cols = grouped.shape
    tile = divisor_tile(cols, 128, 256)
    n, m = len(coefs), 0
    at_col = lambda i: (0, 0, i)
    specs = [pl.BlockSpec(c.shape, lambda i: (0, 0)) for c in coefs]
    whole = (pl.Element(occ), pl.Element(chunk), pl.Element(tile))
    out_specs = [pl.BlockSpec(whole, lambda i: (0, first, i * tile))]
    shapes = [jax.ShapeDtypeStruct((occ, total, cols), F32)]
    scratch = [pltpu.VMEM((chunk, depth) if n > 1 else (8, 128), BF16)]
    args = list(coefs)
    aliases = {}
    if late is not None:
        slots, ids, gammas = late
        m = len(ids)
        args += [slots, *ids, *gammas, grouped]
        specs += [pl.BlockSpec(slots.shape, lambda i: (0, 0))]
        specs += [pl.BlockSpec(v.shape, lambda i: (0, 0)) for v in ids]
        specs += [pl.BlockSpec((g.shape[0], tile), lambda i: (0, i)) for g in gammas]
        specs += [pl.BlockSpec((occ, depth, tile), at_col)]
        out_specs.append(pl.BlockSpec((occ, depth, tile), at_col))
        shapes.append(jax.ShapeDtypeStruct(grouped.shape, BF16))
        scratch.append(pltpu.VMEM((occ * depth, sum(v.shape[1] for v in ids)), BF16))
    else:
        args += [grouped, out]
        specs += [pl.BlockSpec((occ, depth, tile), at_col), pl.BlockSpec(memory_space=pl.ANY)]
        aliases = {len(args) - 1: 0}
    return pl.pallas_call(
        functools.partial(back_kernel, n, m),
        grid=(cols // tile,),
        in_specs=specs,
        out_specs=out_specs,
        out_shape=shapes,
        scratch_shapes=scratch,
        input_output_aliases=aliases,
        compiler_params=params(),
        cost_estimate=pl.CostEstimate(
            flops=1000, bytes_accessed=1000, transcendentals=0
        ),
        name="back_product",
    )(*args)


def tied(value, *after):
    return lax.optimization_barrier((value, *after))[0]


def body(rows, panel, pair_block, resolvent, virt_coef, slot_row):
    high = rows // 2
    up = [(r, (r + 2) % rows) for r in range(rows)]
    down = [(r, (r - 2) % rows) for r in range(rows)]
    swap = [(r, r ^ 1) for r in range(rows)]
    me_row, me_panel = lax.axis_index("rows"), lax.axis_index("panel")
    order = bit_reversed(panel)
    place = me_panel.astype(jnp.int32).reshape(1)
    stages = [1 << k for k in range((panel - 1).bit_length())]

    def over_rows(v, pairs):
        return lax.ppermute(v, "rows", pairs)

    def over_panel(v, width):
        return lax.ppermute(v, "panel", [(q, q ^ width) for q in range(panel)])

    def block_of(s, cross):
        return (me_row // 2 + (high - s)) % high * 2 + ((me_row % 2) ^ cross)

    slots = slot_row.reshape(-1, 1)

    size = pair_block.shape[0]
    step = size // 2

    def row_ids(keys):
        natural = jnp.concatenate(
            [block_of(s, x) * size + c * step + jnp.arange(step, dtype=jnp.int32) for s, x, c in keys]
        )
        cut_ids = natural.reshape(panel, -1)
        return jnp.concatenate([cut_ids[me_panel ^ j] for j in order]).reshape(1, -1)

    parts, sums, owns, gammas, ids = [], [], [], [], []

    def panel_sum(keep, send, keys):
        parts.append(send)
        for k, width in enumerate(stages):
            got = over_panel(send, width)
            if k + 1 < len(stages):
                half = keep.shape[0] // 2
                send = keep[half:] + got[half:]
                keep = (keep[:half], got[:half])
                sums.append(send) if k == 0 else None
                keep = keep[0] + keep[1]
            else:
                keep = keep + got
        own = keep.astype(BF16)
        owns.append(own)
        for width in reversed(stages):
            own = jnp.concatenate([own, over_panel(own, width)], axis=0)
        gammas.append(own)
        ids.append(row_ids(keys))

    def regroup(grouped, which):
        gamma = jnp.concatenate([gammas[k] for k in which], axis=0)
        pick = (slots == jnp.concatenate([ids[k] for k in which], axis=1)).astype(BF16)
        placed = jnp.dot(pick, gamma, preferred_element_type=F32)
        if grouped is not None:
            placed = placed + grouped.astype(F32)
        return placed.astype(BF16)

    piece0 = pair_block[:step]
    piece1 = tied(pair_block, piece0)[step:]
    r16, keep, send = first_product(place, pair_block, resolvent, order)
    panel_sum(keep, send, [(0, 0, 0), (0, 0, 1)])
    grouped = None
    count = 2 * (high - 1) + 1
    batch = max(1, 512 // (2 * step))
    closes = {h for h in range(count) if h >= count - 3 or (h + 1) % batch == 0 or h == count - 4}
    pending = []
    marks = []

    def fence(got):
        h = len(marks)
        after = []
        if h:
            for kind, lag in zip((parts, sums, owns, gammas), LAGS):
                if lag is not None and len(kind) > lag:
                    after.append(kind[-1 - lag])
        got = list(lax.optimization_barrier((*got, *after)))[: len(got)]
        marks.append(got[0])
        return got

    state = {"grouped": None}

    def take(h, items):
        pending.extend(items)
        if h not in closes:
            return
        keep, send = group_product(place, [v for _, v in pending], r16, order)
        panel_sum(keep, send, [key for key, _ in pending])
        pending.clear()
        k = len(gammas) - 1
        if k >= 3 and k % 2:
            state["grouped"] = regroup(state["grouped"], [k - 3, k - 2])

    straight = [{0: piece0, 1: piece1}]
    crossed = []
    h = 0
    for s in range(high - 1):
        straight.append({})
        crossed.append({})
        for c in range(2):
            got = fence([over_rows(straight[s][c], up), over_rows(straight[s][c], swap)])
            straight[s + 1][c], crossed[s][c] = got
            take(h, [((s + 1, 0, c), got[0]), ((s, 1, c), got[1])])
            h += 1
    s = high - 1
    ends = [over_rows(straight[s][0], swap)]
    if high > 1:
        ends.append(over_rows(tied(crossed[0][1], straight[s][0]), down))
    else:
        ends.append(over_rows(straight[s][1], swap))
    ends = fence(ends)
    take(h, [((s, 1, c), ends[c]) for c in range(2)])

    coef_all = lax.all_gather(tied(virt_coef, marks[min(COEF_AT, count - 1)]), "rows", axis=0, tiled=True)
    done = len(gammas) - 2 if len(gammas) % 2 == 0 else len(gammas) - 1
    late = list(range(0 if state["grouped"] is None else done, len(gammas)))
    grouped = state["grouped"]
    if grouped is None:
        grouped = jnp.zeros((slots.shape[0], gammas[0].shape[1]), BF16)

    coef = coef_all.T
    grouped = grouped.reshape(OCC_B, coef.shape[1], -1)
    late_rows = (slots, [ids[k] for k in late], [gammas[k] for k in late])
    return back_product([coef], late_rows, grouped, coef.shape[0], 0, None)[0]


def solution(mesh):
    placed = (P("rows", "panel"), P("panel", "rows"), P("rows", "panel"), P())
    return jax.shard_map(
        functools.partial(body, mesh.shape["rows"], mesh.shape["panel"]),
        mesh=mesh,
        in_specs=placed,
        out_specs=P(None, "panel", "rows"),
        check_vma=False,
    )
```
